1024 devices in a mesh: gx: 32 (over z), gy: 4 (over x), gz: 8 (over y, core).
Axes of the slice: x: 4, y: 4, z: 32, core: 2. Of those that a mesh axis runs over, the one named last changes fastest.
Arguments:
- right_side: float32 [64, 32, 1024], P('gx', 'gy', 'gz'), may hold values from -8 to 8
- stencil: float32 [27, 64, 32, 1024], P(None, 'gx', 'gy', 'gz'), may hold values from -2 to 64, as said below
- cool_table: float32 [256], replicated, may hold values from 0.25 to 4
- cool_bin: int32 [64, 32, 1024], P('gx', 'gy', 'gz'), may hold values from 0 to 254
- cool_frac: float32 [64, 32, 1024], P('gx', 'gy', 'gz'), may hold values from 0 to 1
Outputs:
- solution_field: float32 [64, 32, 1024], P('gx', 'gy', 'gz')
- residual: float32 [64, 32, 1024], P('gx', 'gy', 'gz')
The draws below stay inside these ranges and needn't reach their ends.
Inputs may be any that keep to these rules, and one draw needn't show every extreme that they name: stencil is symmetric: stencil[26 - index] at a cell equals stencil[index] at the cell's neighbour at that index's offset; off-centre entries are not positive and stencil[13] is about 1 plus the sum of their magnitudes.
All inputs are finite; a program needn't handle non-finite values.
Results may differ from the reference program's by a relative error of at most 0.0003.
Values sent between devices are 32-bit elements; how exact they have to be, the bound alone decides.
A program may use at most 32 MiB of HBM per device.

```python
import math
import jax
import jax.numpy as jnp

NBINS = 256
ITERS = 3
NX = 64
NY = 32
NZ = 1024


def draw_stencil(key, part):
    key = jax.random.fold_in(key, 11)
    key_kappa, key_bond = jax.random.split(key)
    shape = (NX, NY, NZ)
    kappa = jnp.exp(jax.random.uniform(key_kappa, shape, jnp.float32, math.log(0.3), math.log(3.0)))
    bonds = jax.random.uniform(key_bond, (13,) + shape, jnp.float32, 0.01, 0.12) * kappa
    lower = []
    mirrored = []
    for index in range(13):
        shift_x = index // 9 - 1
        shift_y = index // 3 % 3 - 1
        shift_z = index % 3 - 1
        lower.append(-bonds[index])
        mirrored.append(-jnp.roll(bonds[index], (shift_x, shift_y, shift_z), (0, 1, 2)))
    centre = 1.0 + jnp.sum(bonds, axis=0) - sum(mirrored)
    upper = [mirrored[26 - index] for index in range(14, 27)]
    return jnp.stack(lower + [centre] + upper).astype(jnp.float32)


def set_ends(entries, stream_key, least, largest):
    index_at = [jax.random.randint(jax.random.fold_in(stream_key, axis), (), 0, length) for axis, length in enumerate(entries.shape)]
    main_axis = entries.shape.index(max(entries.shape))
    beside = index_at[:main_axis] + [(index_at[main_axis] + 1) % entries.shape[main_axis]] + index_at[main_axis + 1:]
    return entries.at[tuple(index_at)].set(least).at[tuple(beside)].set(largest)


def shard_levels(key, dims, pieces, low, high):
    gain = 1.0
    for position, blocks in pieces:
        heights = jax.random.uniform(jax.random.fold_in(jax.random.fold_in(key, 6), position), (blocks,), jnp.float32, low / len(pieces), high / len(pieces))
        gain = gain * jnp.repeat(jnp.exp(heights), dims[position] // blocks).reshape((-1,) + (1,) * (len(dims) - 1 - position))
    return gain


def normal_values(stream_key, shape, width, reach, cuts=(), held_as=jnp.bfloat16):
    values = width * jax.random.normal(stream_key, shape, jnp.float32)
    if cuts:
        values = values * shard_levels(stream_key, shape, cuts, -0.22, 0.18)
    return jnp.clip(values, -reach, reach).astype(held_as)


def setup_inputs(seed: int = 0) -> dict:
    arg_keys = jax.random.split(jax.random.key(seed), 6)
    return {
        "right_side": normal_values(arg_keys[0], (NX, NY, NZ), 1.0, 8.0, ((0, 32), (1, 4), (2, 8)), jnp.float32),
        "stencil": draw_stencil(jax.random.fold_in(arg_keys[5], 71), 0),
        "cool_table": jnp.clip(jnp.exp(jax.random.uniform(arg_keys[2], (NBINS,), jnp.float32, math.log(0.25), math.log(4.0))), 0.25, 4.0),
        "cool_bin": set_ends(jax.random.randint(arg_keys[3], (NX, NY, NZ), 0, NBINS - 1), jax.random.fold_in(arg_keys[3], 1), 0, (NBINS - 1) - 1).astype(jnp.int32),
        "cool_frac": jnp.clip(1.0 * jax.random.uniform(arg_keys[4], (NX, NY, NZ), jnp.float32) ** shard_levels(arg_keys[4], (NX, NY, NZ), ((0, 32), (1, 4), (2, 8)), -0.2, 0.2), 0.0, 1.0),
    }


def cooling_slope(cool_table, cool_bin, cool_frac):
    lower = jnp.take(cool_table, cool_bin)
    upper = jnp.take(cool_table, cool_bin + 1)
    return lower * (1.0 - cool_frac) + upper * cool_frac


def operate(field, stencil, slope):
    total = slope * field
    for index in range(27):
        shift_x = index // 9 - 1
        shift_y = (index // 3) % 3 - 1
        shift_z = index % 3 - 1
        moved = jnp.roll(field, (-shift_x, -shift_y, -shift_z), (0, 1, 2))
        total = total + stencil[index] * moved
    return total


def reference(right_side, stencil, cool_table, cool_bin, cool_frac):
    slope = cooling_slope(cool_table, cool_bin, cool_frac)
    solution_field = jnp.zeros_like(right_side)
    residual = right_side
    direction = right_side
    norm_now = jnp.sum(residual * residual)
    for step in range(ITERS):
        image = operate(direction, stencil, slope)
        alpha = norm_now / jnp.sum(direction * image)
        solution_field = solution_field + alpha * direction
        residual = residual - alpha * image
        norm_next = jnp.sum(residual * residual)
        direction = residual + (norm_next / norm_now) * direction
        norm_now = norm_next
    return solution_field, residual
```

```python
import functools
import jax
import jax.numpy as jnp
from jax import lax
from jax.experimental import pallas as pl
from jax.experimental.pallas import tpu as pltpu
from jax.sharding import PartitionSpec as P

MESH = pl.DeviceIdType.MESH
GX, GY, GZ = 32, 4, 8
PLANE = GY * GZ
SHIFT = 4.5
OFFSETS = [
    (a, b, c)
    for a in (-1, 0, 1)
    for b in (-1, 0, 1)
    for c in (-1, 0, 1)
    if (a, b, c) != (0, 0, 0)
]


def two_sum(a, b):
    total = a + b
    part = total - a
    return total, (a - (total - part)) + (b - part)


def pair_add(x, y):
    total, error = two_sum(x[0], y[0])
    error = error + (x[1] + y[1])
    high = total + error
    return high, error - (high - total)


def halves(a):
    big = a * 4097.0
    high = big - (big - a)
    return high, a - high


def pair_minus_scaled(x, y, scale, scale_halves):
    product = y[0] * scale
    high, low = halves(y[0])
    scale_high, scale_low = scale_halves
    error = high * scale_high - product
    error = error + high * scale_low
    error = error + low * scale_high
    error = error + low * scale_low
    error = error + y[1] * scale
    return pair_add(x, (-product, -error))


def conjugate(moments):
    tau = moments[1][0] / moments[0][0]
    tau_halves = halves(tau)
    level = list(moments)
    shifted = [level[0][0]]
    while len(level) > 1:
        level = [
            pair_minus_scaled(level[k + 1], level[k], tau, tau_halves)
            for k in range(len(level) - 1)
        ]
        shifted.append(level[0][0])
    m = shifted
    s = tau + SHIFT

    def form(p, q):
        total = None
        for i, u in enumerate(p):
            inner = None
            for j, w in enumerate(q):
                term = w * m[i + j]
                inner = term if inner is None else inner + term
            total = u * inner if total is None else total + u * inner
        return total

    def image_of(p):
        out = [s * p[0]]
        for i in range(1, len(p)):
            out.append(p[i - 1] + s * p[i])
        out.append(p[-1])
        return out

    bottom = s * m[0] + m[1]
    alpha = m[0] / bottom
    x = [alpha]
    r = [m[1] / bottom, -alpha]
    norm = form(r, r)
    beta = norm / m[0]
    d = [r[0] + beta, r[1]]
    for step in (1, 2):
        image = image_of(d)
        alpha = norm / form(d, image)
        x = [x[i] + alpha * d[i] if i < len(x) else alpha * d[i] for i in range(len(d))]
        r = [r[i] - alpha * image[i] if i < len(r) else -alpha * image[i] for i in range(len(image))]
        if step == 1:
            new = form(r, r)
            beta = new / norm
            d = [r[i] + beta * d[i] if i < len(d) else r[i] for i in range(len(r))]
            norm = new
    return tau, x, r


def kernel(
    rhs_hbm, stencil_hbm, table_hbm, bin_hbm, frac_hbm, x_out, r_out,
    st, halo, table, bins, frac, plane_rows, line_rows,
    in_sem, send_sem, halo_sem, plane_sem, line_sem, halo_bytes,
):
    gx, gy, gz = lax.axis_index("gx"), lax.axis_index("gy"), lax.axis_index("gz")

    def at(dx, dy, dz):
        return (
            lax.rem(gx + (dx + GX), GX),
            lax.rem(gy + (dy + GY), GY),
            lax.rem(gz + (dz + GZ), GZ),
        )

    loads = [
        pltpu.make_async_copy(rhs_hbm, halo.at[0, 0:2, 0, 0:8, :], in_sem.at[0]),
        pltpu.make_async_copy(stencil_hbm, st, in_sem.at[1]),
        pltpu.make_async_copy(table_hbm, table, in_sem.at[2]),
        pltpu.make_async_copy(bin_hbm, bins, in_sem.at[3]),
        pltpu.make_async_copy(frac_hbm, frac, in_sem.at[4]),
    ]
    for load in loads:
        load.start()

    plane_offsets = [(0, b, c) for b in range(GY) for c in range(GZ) if (b, c) != (0, 0)]
    line_offsets = [(a, 0, 0) for a in [16] + [k * e for k in range(15, 0, -1) for e in (1, -1)]]
    partners = line_offsets + [o for o in OFFSETS if o[0] != 0 and (o[1], o[2]) != (0, 0)] + plane_offsets
    barrier = pltpu.get_barrier_semaphore()
    for o in partners:
        pl.semaphore_signal(barrier, inc=1, device_id=at(*o), device_id_type=MESH)

    for load in loads:
        load.wait()

    low_tab = jnp.broadcast_to(table[0:1, :], (8, 128))
    high_tab = jnp.broadcast_to(table[1:2, :], (8, 128))

    def look(index):
        lane = index & 127
        low = jnp.take_along_axis(low_tab, lane, axis=1, mode="promise_in_bounds")
        high = jnp.take_along_axis(high_tab, lane, axis=1, mode="promise_in_bounds")
        return jnp.where(index >= 128, high, low)

    for p in range(2):
        slope = look(bins[p]) * (1.0 - frac[p]) + look(bins[p] + 1) * frac[p]
        st[13, p] = st[13, p] + (slope - SHIFT)

    pl.semaphore_wait(barrier, len(partners))

    lane = lax.broadcasted_iota(jnp.int32, (16, 128), 1)
    from_right = lane < 64

    def exchange(it):
        for dx, dy, dz in OFFSETS:
            src_p, dst_p, n_p = {0: (0, 0, 2), 1: (1, 3, 1), -1: (0, 2, 1)}[dx]
            src_y, dst_y, n_y = {0: (0, 0, 8), 1: (7, 15, 1), -1: (0, 8, 1)}[dy]
            side = {0: 0, 1: 2, -1: 1}[dz]
            pltpu.make_async_remote_copy(
                src_ref=halo.at[it, pl.ds(src_p, n_p), 0, pl.ds(src_y, n_y), :],
                dst_ref=halo.at[it, pl.ds(dst_p, n_p), side, pl.ds(dst_y, n_y), :],
                send_sem=send_sem.at[0],
                recv_sem=halo_sem.at[it],
                device_id=at(dx, dy, dz),
                device_id_type=MESH,
            ).start()
        pltpu.make_async_copy(halo_bytes, halo_bytes, halo_sem.at[it]).wait()

    def apply(it):
        total = [jnp.zeros((8, 128), jnp.float32) for _ in range(2)]
        for slot, plane in ((0, 0), (1, 1), (2, 2), (3, -1)):
            side = jnp.where(from_right, halo[it, slot, 1], halo[it, slot, 2])
            wide = jnp.concatenate([halo[it, slot, 0], side], axis=1)
            for b in (-1, 0, 1):
                rows = wide if b == 0 else pltpu.roll(wide, (-b) % 16, 0)
                rows = rows[0:8]
                for c in (-1, 0, 1):
                    moved = rows if c == 0 else pltpu.roll(rows, (-c) % 256, 1)
                    moved = moved[:, 0:128]
                    for p in range(2):
                        a = plane - p
                        if -1 <= a <= 1:
                            total[p] = total[p] + st[9 * (a + 1) + 3 * (b + 1) + (c + 1), p] * moved
        return total

    v = [[halo[0, p, 0, 0:8, :] for p in range(2)]]
    for it in range(3):
        exchange(it)
        new = apply(it)
        if it < 2:
            for p in range(2):
                halo[it + 1, p, 0, 0:8, :] = new[p]
        v.append(new)

    row_id = lax.broadcasted_iota(jnp.int32, (8, 128), 0)
    lane_id = lax.broadcasted_iota(jnp.int32, (8, 128), 1)
    tile = jnp.zeros((8, 128), jnp.float32)
    for k in range(6):
        i, j = k // 2, (k + 1) // 2
        product = v[i][0] * v[j][0] + v[i][1] * v[j][1]
        tile = jnp.where(row_id == k, jnp.sum(product, axis=0, keepdims=True), tile)
    for shift in (64, 32, 16):
        tile = tile + pltpu.roll(tile, shift, 1)
    row = jnp.sum(jnp.where((lane_id >> 4) == row_id, tile, 0.0), axis=0, keepdims=True)

    def spread(rows, here, offsets, sem):
        for o in offsets:
            pltpu.make_async_remote_copy(
                src_ref=rows.at[here],
                dst_ref=rows.at[here],
                send_sem=send_sem.at[0],
                recv_sem=sem,
                device_id=at(*o),
                device_id_type=MESH,
            ).start()
        count = len(offsets)
        pltpu.make_async_copy(rows.at[0:count], rows.at[0:count], sem).wait()

    here = gy * GZ + gz
    plane_rows[here] = row
    spread(plane_rows, here, plane_offsets, plane_sem.at[0])
    terms = [plane_rows[k] for k in range(PLANE)]
    while len(terms) > 1:
        terms = [terms[k] + terms[k + 1] for k in range(0, len(terms), 2)]
    line_rows[gx] = terms[0]
    spread(line_rows, gx, line_offsets, line_sem.at[0])
    terms = [(line_rows[k], None) for k in range(GX)]
    terms = [two_sum(terms[k][0], terms[k + 1][0]) for k in range(0, GX, 2)]
    while len(terms) > 1:
        terms = [pair_add(terms[k], terms[k + 1]) for k in range(0, len(terms), 2)]
    pair = terms[0]
    for shift in (8, 4, 2, 1):
        pair = pair_add(pair, (pltpu.roll(pair[0], shift, 1), pltpu.roll(pair[1], shift, 1)))

    moments = [
        tuple(jnp.broadcast_to(part[:, 16 * k + 15 : 16 * k + 16], (8, 128)) for part in pair)
        for k in range(6)
    ]
    tau, x_coef, r_coef = conjugate(moments)
    for p in range(2):
        level = [v[k][p] for k in range(4)]
        basis = [level[0]]
        while len(level) > 1:
            level = [level[k + 1] - tau * level[k] for k in range(len(level) - 1)]
            basis.append(level[0])
        x_out[p] = x_coef[0] * basis[0] + x_coef[1] * basis[1] + x_coef[2] * basis[2]
        r_out[p] = (
            r_coef[0] * basis[0] + r_coef[1] * basis[1] + r_coef[2] * basis[2] + r_coef[3] * basis[3]
        )

    for it in range(3):
        pltpu.make_async_copy(halo_bytes, halo_bytes, send_sem.at[0]).wait()
    for rows, count in ((plane_rows, PLANE - 1), (line_rows, GX - 1)):
        pltpu.make_async_copy(rows.at[0:count], rows.at[0:count], send_sem.at[0]).wait()


def local(right_side, stencil, cool_table, cool_bin, cool_frac):
    block = jax.ShapeDtypeStruct((2, 8, 128), jnp.float32)
    return pl.pallas_call(
        kernel,
        out_shape=(block, block),
        in_specs=[pl.BlockSpec(memory_space=pl.ANY)] * 5,
        out_specs=[pl.BlockSpec(memory_space=pltpu.VMEM)] * 2,
        scratch_shapes=[
            pltpu.VMEM((27, 2, 8, 128), jnp.float32),
            pltpu.VMEM((3, 4, 3, 16, 128), jnp.float32),
            pltpu.VMEM((2, 128), jnp.float32),
            pltpu.VMEM((2, 8, 128), jnp.int32),
            pltpu.VMEM((2, 8, 128), jnp.float32),
            pltpu.VMEM((PLANE, 1, 128), jnp.float32),
            pltpu.VMEM((GX, 1, 128), jnp.float32),
            pltpu.SemaphoreType.DMA((5,)),
            pltpu.SemaphoreType.DMA((1,)),
            pltpu.SemaphoreType.DMA((3,)),
            pltpu.SemaphoreType.DMA((1,)),
            pltpu.SemaphoreType.DMA((1,)),
            pltpu.VMEM((104, 128), jnp.float32),
        ],
        compiler_params=pltpu.CompilerParams(
            collective_id=0, has_side_effects=True, vmem_limit_bytes=60 << 20
        ),
    )(right_side, stencil, cool_table.reshape(2, 128), cool_bin, cool_frac)


def solution(mesh):
    block = P("gx", "gy", "gz")
    return jax.shard_map(
        local,
        mesh=mesh,
        in_specs=(block, P(None, "gx", "gy", "gz"), P(), block, block),
        out_specs=(block, block),
        check_vma=False,
    )
```

```python
import functools
import jax
import jax.numpy as jnp
from jax import lax
from jax.experimental import pallas as pl
from jax.experimental.pallas import tpu as pltpu
from jax.sharding import PartitionSpec as P

MESH = pl.DeviceIdType.MESH
GX, GY, GZ = 32, 4, 8
PLANE = GY * GZ
SHIFT = 4.5
NEAR = [(b, c) for b in (-1, 0, 1) for c in (-1, 0, 1)]
FIELD_ROWS = {0: (0, 0, 8), 1: (5, 13, 3), -1: (0, 8, 3)}
COEF_ROWS = {0: (0, 0, 8), 1: (6, 14, 2), -1: (0, 8, 2)}
FIELD_PLANES = {0: (3, 3, 2), 1: (3, 1, 2), -1: (3, 5, 2), 2: (4, 0, 1), -2: (3, 7, 1)}
COEF_PLANES = {0: (2, 2), 1: (2, 0), -1: (2, 4)}
SIDE = {0: 0, 1: 2, -1: 1}


def two_sum(a, b):
    total = a + b
    part = total - a
    return total, (a - (total - part)) + (b - part)


def pair_add(x, y):
    total, error = two_sum(x[0], y[0])
    error = error + (x[1] + y[1])
    high = total + error
    return high, error - (high - total)


def halves(a):
    big = a * 4097.0
    high = big - (big - a)
    return high, a - high


def pair_minus_scaled(x, y, scale, scale_halves):
    product = y[0] * scale
    high, low = halves(y[0])
    scale_high, scale_low = scale_halves
    error = high * scale_high - product
    error = error + high * scale_low
    error = error + low * scale_high
    error = error + low * scale_low
    error = error + y[1] * scale
    return pair_add(x, (-product, -error))


def conjugate(moments):
    tau = moments[1][0] / moments[0][0]
    tau_halves = halves(tau)
    level = list(moments)
    shifted = [level[0][0]]
    while len(level) > 1:
        level = [
            pair_minus_scaled(level[k + 1], level[k], tau, tau_halves)
            for k in range(len(level) - 1)
        ]
        shifted.append(level[0][0])
    m = shifted
    s = tau + SHIFT

    def form(p, q):
        total = None
        for i, u in enumerate(p):
            inner = None
            for j, w in enumerate(q):
                term = w * m[i + j]
                inner = term if inner is None else inner + term
            total = u * inner if total is None else total + u * inner
        return total

    def image_of(p):
        out = [s * p[0]]
        for i in range(1, len(p)):
            out.append(p[i - 1] + s * p[i])
        out.append(p[-1])
        return out

    bottom = s * m[0] + m[1]
    alpha = m[0] / bottom
    x = [alpha]
    r = [m[1] / bottom, -alpha]
    norm = form(r, r)
    beta = norm / m[0]
    d = [r[0] + beta, r[1]]
    for step in (1, 2):
        image = image_of(d)
        alpha = norm / form(d, image)
        x = [x[i] + alpha * d[i] if i < len(x) else alpha * d[i] for i in range(len(d))]
        r = [r[i] - alpha * image[i] if i < len(r) else -alpha * image[i] for i in range(len(image))]
        if step == 1:
            new = form(r, r)
            beta = new / norm
            d = [r[i] + beta * d[i] if i < len(d) else r[i] for i in range(len(r))]
            norm = new
    return tau, x, r


def kernel(
    rhs_hbm, stencil_hbm, table_hbm, bin_hbm, frac_hbm, x_out, r_out,
    coef, packed, edge, field, moved, table, bins, frac, plane_rows, line_rows,
    in_sem, send_sem, field_sem, edge_sem, coef_sem, face_sem, plane_sem, line_sem,
):
    gx, gy, gz = lax.axis_index("gx"), lax.axis_index("gy"), lax.axis_index("gz")

    def at(dx, dy, dz):
        return (
            lax.rem(gx + (dx + GX), GX),
            lax.rem(gy + (dy + GY), GY),
            lax.rem(gz + (dz + GZ), GZ),
        )

    loads = [
        pltpu.make_async_copy(rhs_hbm, field.at[0, 3:5, 0:8, :], in_sem.at[0]),
        pltpu.make_async_copy(stencil_hbm, coef.at[:, 2:4, 0:8, 0:128], in_sem.at[1]),
        pltpu.make_async_copy(table_hbm, table, in_sem.at[2]),
        pltpu.make_async_copy(bin_hbm, bins, in_sem.at[3]),
        pltpu.make_async_copy(frac_hbm, frac, in_sem.at[4]),
    ]
    for load in loads:
        load.start()

    plane_offsets = [(0, b, c) for b in range(GY) for c in range(GZ) if (b, c) != (0, 0)]
    line_offsets = [(a, 0, 0) for a in [16] + [k * e for k in range(15, 0, -1) for e in (1, -1)]]
    partners = (
        line_offsets
        + [(a, b, c) for a in (-2, 2, -1, 1) for b, c in NEAR if (b, c) != (0, 0)]
        + plane_offsets
    )
    barrier = pltpu.get_barrier_semaphore()
    for o in partners:
        pl.semaphore_signal(barrier, inc=1, device_id=at(*o), device_id_type=MESH)

    for load in loads:
        load.wait()

    low_tab = jnp.broadcast_to(table[0:1, :], (8, 128))
    high_tab = jnp.broadcast_to(table[1:2, :], (8, 128))

    def look(index):
        lane = index & 127
        low = jnp.take_along_axis(low_tab, lane, axis=1, mode="promise_in_bounds")
        high = jnp.take_along_axis(high_tab, lane, axis=1, mode="promise_in_bounds")
        return jnp.where(index >= 128, high, low)

    row_id = lax.broadcasted_iota(jnp.int32, (8, 128), 0)
    lane_id = lax.broadcasted_iota(jnp.int32, (8, 128), 1)
    for p in range(2):
        slope = look(bins[p]) * (1.0 - frac[p]) + look(bins[p] + 1) * frac[p]
        coef[13, 2 + p, 0:8, 0:128] = coef[13, 2 + p, 0:8, 0:128] + (slope - SHIFT)
        tile = jnp.zeros((8, 128), jnp.float32)
        for k in range(27):
            turned = pltpu.roll(coef[k, 2 + p, 0:8, 0:128], (4 * k + 2) % 128, 1)
            tile = jnp.where((lane_id >> 2) == k, turned, tile)
        packed[p] = tile

    pl.semaphore_wait(barrier, len(partners))

    def send(src, dst, sem, o):
        pltpu.make_async_remote_copy(
            src_ref=src, dst_ref=dst, send_sem=send_sem.at[0], recv_sem=sem,
            device_id=at(*o), device_id_type=MESH,
        ).start()

    def send_field(dx, dy, dz):
        p_src, p_dst, p_n = FIELD_PLANES[dx]
        y_src, y_dst, y_n = FIELD_ROWS[dy]
        send(
            field.at[0, pl.ds(p_src, p_n), pl.ds(y_src, y_n), :],
            field.at[SIDE[dz], pl.ds(p_dst, p_n), pl.ds(y_dst, y_n), :],
            field_sem.at[0], (dx, dy, dz),
        )

    def send_edge(dx, dy, dz):
        p_src, p_dst = COEF_PLANES[dx]
        y_src, y_dst, y_n = COEF_ROWS[dy]
        send(
            packed.at[:, pl.ds(y_src, y_n), :],
            edge.at[SIDE[dz] - 1, pl.ds(p_dst, 2), pl.ds(y_dst, y_n), :],
            edge_sem.at[0], (dx, dy, dz),
        )

    def send_coef(dx, dy, first, count, sem):
        p_src, p_dst = COEF_PLANES[dx]
        y_src, y_dst, y_n = COEF_ROWS[dy]
        send(
            coef.at[pl.ds(first, count), pl.ds(p_src, 2), pl.ds(y_src, y_n), 0:128],
            coef.at[pl.ds(first, count), pl.ds(p_dst, 2), pl.ds(y_dst, y_n), 0:128],
            sem, (dx, dy, 0),
        )

    offsets = [(a, b, c) for a in (-1, 1, -2, 2, 0) for b, c in NEAR if (a, b, c) != (0, 0, 0)]
    offsets.sort(key=lambda o: -sum(abs(d) for d in o))
    for o in offsets:
        send_field(*o)
        if o[2] != 0 and abs(o[0]) <= 1:
            send_edge(*o)
    for dx in (-1, 1):
        for dy in (-1, 1):
            send_coef(dx, dy, 0, 27, coef_sem.at[0])
    send_coef(1, 0, 0, 14, face_sem.at[0])
    send_coef(-1, 0, 13, 14, face_sem.at[0])
    for dy in (-1, 1):
        send_coef(0, dy, 0, 27, coef_sem.at[0])

    field_bytes = coef.at[0:20, 0, :, 0:128]
    edge_bytes = coef.at[0:9, 0, :, 0:128]
    coef_bytes = coef.at[0:27, 0:3, 0:8, 0:128]
    face_bytes = coef.at[0:14, 0:2, :, 0:128]

    def moved_by(array, b, c):
        if b:
            array = pltpu.roll(array, (-b) % 16, 1)
        if c:
            array = pltpu.roll(array, (-c) % 256, 2)
        return array

    def turn(array, planes):
        for n, (b, c) in enumerate(NEAR):
            moved[n, 0:planes] = moved_by(array, b, c)

    def apply(planes, first):
        total = jnp.zeros((planes, 16, 256), jnp.float32)
        for k in range(27):
            a = k // 9
            total = total + coef[k, first : first + planes] * moved[k % 9, a : a + planes]
        return total

    pltpu.make_async_copy(field_bytes, field_bytes, field_sem.at[0]).wait()
    lane_wide = lax.broadcasted_iota(jnp.int32, (8, 16, 128), 2)
    side = jnp.where(lane_wide < 64, field[1], field[2])
    turn(jnp.concatenate([field[0], side], axis=2), 8)

    pltpu.make_async_copy(edge_bytes, edge_bytes, edge_sem.at[0]).wait()
    merged = jnp.where((lane_wide[0:6] & 3) < 2, edge[1], edge[0])
    for k in range(27):
        coef[k, :, :, 128:256] = pltpu.roll(merged, (126 - 4 * k) % 128, 2)

    pltpu.make_async_copy(coef_bytes, coef_bytes, coef_sem.at[0]).wait()
    pltpu.make_async_copy(face_bytes, face_bytes, face_sem.at[0]).wait()
    for k in range(27):
        if k == 13:
            continue
        a, b, c = k // 9 - 1, k // 3 % 3 - 1, k % 3 - 1
        first = 0 if k > 13 else 4
        mirror = moved_by(coef[26 - k, first + a : first + a + 2], b, c)
        coef[k, first : first + 2, 0:8, 0:128] = mirror[:, 0:8, 0:128]

    one = apply(6, 0)
    turn(one, 6)
    two = apply(4, 1)
    turn(two, 4)
    three = jnp.zeros((2, 8, 128), jnp.float32)
    for k in range(27):
        a = k // 9
        three = three + coef[k, 2:4, 0:8, 0:128] * moved[k % 9, a : a + 2, 0:8, 0:128]
    own = [field[0, 3:5, 0:8, :], one[2:4, 0:8, 0:128], two[1:3, 0:8, 0:128], three]
    v = [[array[p] for p in range(2)] for array in own]

    tile = jnp.zeros((8, 128), jnp.float32)
    for k in range(6):
        i, j = k // 2, (k + 1) // 2
        product = v[i][0] * v[j][0] + v[i][1] * v[j][1]
        tile = jnp.where(row_id == k, jnp.sum(product, axis=0, keepdims=True), tile)
    for shift in (64, 32, 16):
        tile = tile + pltpu.roll(tile, shift, 1)
    row = jnp.sum(jnp.where((lane_id >> 4) == row_id, tile, 0.0), axis=0, keepdims=True)

    def spread(rows, here, offsets, sem):
        for o in offsets:
            pltpu.make_async_remote_copy(
                src_ref=rows.at[here],
                dst_ref=rows.at[here],
                send_sem=send_sem.at[0],
                recv_sem=sem,
                device_id=at(*o),
                device_id_type=MESH,
            ).start()
        count = len(offsets)
        pltpu.make_async_copy(rows.at[0:count], rows.at[0:count], sem).wait()

    here = gy * GZ + gz
    plane_rows[here] = row
    spread(plane_rows, here, plane_offsets, plane_sem.at[0])
    terms = [plane_rows[k] for k in range(PLANE)]
    while len(terms) > 1:
        terms = [terms[k] + terms[k + 1] for k in range(0, len(terms), 2)]
    line_rows[gx] = terms[0]
    spread(line_rows, gx, line_offsets, line_sem.at[0])
    terms = [(line_rows[k], None) for k in range(GX)]
    terms = [two_sum(terms[k][0], terms[k + 1][0]) for k in range(0, GX, 2)]
    while len(terms) > 1:
        terms = [pair_add(terms[k], terms[k + 1]) for k in range(0, len(terms), 2)]
    pair = terms[0]
    for shift in (8, 4, 2, 1):
        pair = pair_add(pair, (pltpu.roll(pair[0], shift, 1), pltpu.roll(pair[1], shift, 1)))

    moments = [
        tuple(jnp.broadcast_to(part[:, 16 * k + 15 : 16 * k + 16], (8, 128)) for part in pair)
        for k in range(6)
    ]
    tau, x_coef, r_coef = conjugate(moments)
    for p in range(2):
        level = [v[k][p] for k in range(4)]
        basis = [level[0]]
        while len(level) > 1:
            level = [level[k + 1] - tau * level[k] for k in range(len(level) - 1)]
            basis.append(level[0])
        x_out[p] = x_coef[0] * basis[0] + x_coef[1] * basis[1] + x_coef[2] * basis[2]
        r_out[p] = (
            r_coef[0] * basis[0] + r_coef[1] * basis[1] + r_coef[2] * basis[2] + r_coef[3] * basis[3]
        )

    for size in (field_bytes, edge_bytes, coef_bytes, face_bytes):
        pltpu.make_async_copy(size, size, send_sem.at[0]).wait()
    for rows, count in ((plane_rows, PLANE - 1), (line_rows, GX - 1)):
        pltpu.make_async_copy(rows.at[0:count], rows.at[0:count], send_sem.at[0]).wait()


def local(right_side, stencil, cool_table, cool_bin, cool_frac):
    block = jax.ShapeDtypeStruct((2, 8, 128), jnp.float32)
    return pl.pallas_call(
        kernel,
        out_shape=(block, block),
        in_specs=[pl.BlockSpec(memory_space=pl.ANY)] * 5,
        out_specs=[pl.BlockSpec(memory_space=pltpu.VMEM)] * 2,
        scratch_shapes=[
            pltpu.VMEM((27, 6, 16, 256), jnp.float32),
            pltpu.VMEM((2, 8, 128), jnp.float32),
            pltpu.VMEM((2, 6, 16, 128), jnp.float32),
            pltpu.VMEM((3, 8, 16, 128), jnp.float32),
            pltpu.VMEM((9, 8, 16, 256), jnp.float32),
            pltpu.VMEM((2, 128), jnp.float32),
            pltpu.VMEM((2, 8, 128), jnp.int32),
            pltpu.VMEM((2, 8, 128), jnp.float32),
            pltpu.VMEM((PLANE, 1, 128), jnp.float32),
            pltpu.VMEM((GX, 1, 128), jnp.float32),
            pltpu.SemaphoreType.DMA((5,)),
        ]
        + [pltpu.SemaphoreType.DMA((1,))] * 7,
        compiler_params=pltpu.CompilerParams(
            collective_id=0, has_side_effects=True, vmem_limit_bytes=60 << 20
        ),
    )(right_side, stencil, cool_table.reshape(2, 128), cool_bin, cool_frac)


def solution(mesh):
    block = P("gx", "gy", "gz")
    return jax.shard_map(
        local,
        mesh=mesh,
        in_specs=(block, P(None, "gx", "gy", "gz"), P(), block, block),
        out_specs=(block, block),
        check_vma=False,
    )
```

```python
import functools
import jax
import jax.numpy as jnp
from jax import lax
from jax.experimental import pallas as pl
from jax.experimental.pallas import tpu as pltpu
from jax.sharding import PartitionSpec as P

MESH = pl.DeviceIdType.MESH
GX, GY, GZ = 32, 4, 8
PLANE = GY * GZ
SHIFT = 4.5
NEAR = [(b, c) for b in (-1, 0, 1) for c in (-1, 0, 1)]
FIELD_ROWS = {0: (0, 0, 8), 1: (5, 13, 3), -1: (0, 8, 3)}
COEF_ROWS = {0: (0, 0, 8), 1: (6, 14, 2), -1: (0, 8, 2)}
FIELD_PLANES = {0: (3, 3, 2), 1: (3, 1, 2), -1: (3, 5, 2), 2: (4, 0, 1), -2: (3, 7, 1)}
COEF_PLANES = {0: (2, 2), 1: (2, 0), -1: (2, 4)}
SIDE = {0: 0, 1: 2, -1: 1}


def two_sum(a, b):
    total = a + b
    part = total - a
    return total, (a - (total - part)) + (b - part)


def pair_add(x, y):
    total, error = two_sum(x[0], y[0])
    error = error + (x[1] + y[1])
    high = total + error
    return high, error - (high - total)


def halves(a):
    big = a * 4097.0
    high = big - (big - a)
    return high, a - high


def pair_minus_scaled(x, y, scale, scale_halves):
    product = y[0] * scale
    high, low = halves(y[0])
    scale_high, scale_low = scale_halves
    error = high * scale_high - product
    error = error + high * scale_low
    error = error + low * scale_high
    error = error + low * scale_low
    error = error + y[1] * scale
    return pair_add(x, (-product, -error))


def conjugate(moments):
    tau = moments[1][0] / moments[0][0]
    tau_halves = halves(tau)
    level = list(moments)
    shifted = [level[0][0]]
    while len(level) > 1:
        level = [
            pair_minus_scaled(level[k + 1], level[k], tau, tau_halves)
            for k in range(len(level) - 1)
        ]
        shifted.append(level[0][0])
    m = shifted
    s = tau + SHIFT

    def form(p, q):
        total = None
        for i, u in enumerate(p):
            inner = None
            for j, w in enumerate(q):
                term = w * m[i + j]
                inner = term if inner is None else inner + term
            total = u * inner if total is None else total + u * inner
        return total

    def image_of(p):
        out = [s * p[0]]
        for i in range(1, len(p)):
            out.append(p[i - 1] + s * p[i])
        out.append(p[-1])
        return out

    bottom = s * m[0] + m[1]
    alpha = m[0] / bottom
    x = [alpha]
    r = [m[1] / bottom, -alpha]
    norm = form(r, r)
    beta = norm / m[0]
    d = [r[0] + beta, r[1]]
    for step in (1, 2):
        image = image_of(d)
        alpha = norm / form(d, image)
        x = [x[i] + alpha * d[i] if i < len(x) else alpha * d[i] for i in range(len(d))]
        r = [r[i] - alpha * image[i] if i < len(r) else -alpha * image[i] for i in range(len(image))]
        if step == 1:
            new = form(r, r)
            beta = new / norm
            d = [r[i] + beta * d[i] if i < len(d) else r[i] for i in range(len(r))]
            norm = new
    return tau, x, r


def kernel(
    rhs_hbm, stencil_hbm, table_hbm, bin_hbm, frac_hbm, out,
    coef, packed, edge, field, moved, table, bins, frac, plane_rows, line_rows,
    in_sem, send_sem, field_sem, edge_sem, coef_sem, face_sem, plane_sem, line_sem,
    relay_4, relay_8,
):
    gx, gy, gz = lax.axis_index("gx"), lax.axis_index("gy"), lax.axis_index("gz")

    def at(dx, dy, dz):
        return (
            lax.rem(gx + (dx + GX), GX),
            lax.rem(gy + (dy + GY), GY),
            lax.rem(gz + (dz + GZ), GZ),
        )

    loads = [
        pltpu.make_async_copy(rhs_hbm, field.at[0, 3:5, 0:8, :], in_sem.at[0]),
        pltpu.make_async_copy(stencil_hbm, coef.at[:, 2:4, 0:8, 0:128], in_sem.at[1]),
        pltpu.make_async_copy(table_hbm, table, in_sem.at[2]),
        pltpu.make_async_copy(bin_hbm, bins, in_sem.at[3]),
        pltpu.make_async_copy(frac_hbm, frac, in_sem.at[4]),
    ]
    for load in loads:
        load.start()

    plane_offsets = [(0, b, c) for b in range(GY) for c in range(GZ) if (b, c) != (0, 0)]
    line_offsets = [(a, 0, 0) for a in [16] + [k * e for k in range(15, 0, -1) for e in (1, -1)]]
    around = [(a, b, c) for a in (-2, 2, -1, 1) for b, c in NEAR if (b, c) != (0, 0)]
    around.sort(key=lambda o: -sum(abs(d) for d in o))
    partners = around + plane_offsets + [(a, 0, 0) for a in (4, -4, 3, -3, 2, -2, 1, -1)]
    barrier = pltpu.get_barrier_semaphore()
    for o in partners:
        pl.semaphore_signal(barrier, inc=1, device_id=at(*o), device_id_type=MESH)

    for load in loads:
        load.wait()

    low_tab = jnp.broadcast_to(table[0:1, :], (8, 128))
    high_tab = jnp.broadcast_to(table[1:2, :], (8, 128))

    def look(index):
        lane = index & 127
        low = jnp.take_along_axis(low_tab, lane, axis=1, mode="promise_in_bounds")
        high = jnp.take_along_axis(high_tab, lane, axis=1, mode="promise_in_bounds")
        return jnp.where(index >= 128, high, low)

    row_id = lax.broadcasted_iota(jnp.int32, (8, 128), 0)
    lane_id = lax.broadcasted_iota(jnp.int32, (8, 128), 1)
    for p in range(2):
        slope = look(bins[p]) * (1.0 - frac[p]) + look(bins[p] + 1) * frac[p]
        coef[13, 2 + p, 0:8, 0:128] = coef[13, 2 + p, 0:8, 0:128] + (slope - SHIFT)
        tile = jnp.zeros((8, 128), jnp.float32)
        for k in range(27):
            turned = pltpu.roll(coef[k, 2 + p, 0:8, 0:128], (4 * k + 2) % 128, 1)
            tile = jnp.where((lane_id >> 2) == k, turned, tile)
        packed[p] = tile

    pl.semaphore_wait(barrier, len(partners))

    for a in (4, -4):
        pl.semaphore_signal(relay_4, inc=1, device_id=at(a, 0, 0), device_id_type=MESH)

    def send(src, dst, sem, o):
        pltpu.make_async_remote_copy(
            src_ref=src, dst_ref=dst, send_sem=send_sem.at[0], recv_sem=sem,
            device_id=at(*o), device_id_type=MESH,
        ).start()

    def send_field(dx, dy, dz):
        p_src, p_dst, p_n = FIELD_PLANES[dx]
        y_src, y_dst, y_n = FIELD_ROWS[dy]
        send(
            field.at[0, pl.ds(p_src, p_n), pl.ds(y_src, y_n), :],
            field.at[SIDE[dz], pl.ds(p_dst, p_n), pl.ds(y_dst, y_n), :],
            field_sem.at[0], (dx, dy, dz),
        )

    def send_edge(dx, dy, dz):
        p_src, p_dst = COEF_PLANES[dx]
        y_src, y_dst, y_n = COEF_ROWS[dy]
        send(
            packed.at[:, pl.ds(y_src, y_n), :],
            edge.at[SIDE[dz] - 1, pl.ds(p_dst, 2), pl.ds(y_dst, y_n), :],
            edge_sem.at[0], (dx, dy, dz),
        )

    def send_coef(dx, dy, first, count, sem):
        p_src, p_dst = COEF_PLANES[dx]
        y_src, y_dst, y_n = COEF_ROWS[dy]
        send(
            coef.at[pl.ds(first, count), pl.ds(p_src, 2), pl.ds(y_src, y_n), 0:128],
            coef.at[pl.ds(first, count), pl.ds(p_dst, 2), pl.ds(y_dst, y_n), 0:128],
            sem, (dx, dy, 0),
        )

    offsets = [(a, b, c) for a in (-1, 1, -2, 2, 0) for b, c in NEAR if (a, b, c) != (0, 0, 0)]
    offsets.sort(key=lambda o: -sum(abs(d) for d in o))
    for o in offsets:
        send_field(*o)
        if o[2] != 0 and abs(o[0]) <= 1:
            send_edge(*o)
    for dx in (-1, 1):
        for dy in (-1, 1):
            send_coef(dx, dy, 0, 27, coef_sem.at[0])
    send_coef(1, 0, 0, 14, face_sem.at[0])
    send_coef(-1, 0, 13, 14, face_sem.at[0])
    for dy in (-1, 1):
        send_coef(0, dy, 0, 27, coef_sem.at[0])

    pl.semaphore_wait(relay_4, 2)
    for a in (8, -8):
        pl.semaphore_signal(relay_8, inc=1, device_id=at(a, 0, 0), device_id_type=MESH)

    field_bytes = coef.at[0:20, 0, :, 0:128]
    edge_bytes = coef.at[0:9, 0, :, 0:128]
    coef_bytes = coef.at[0:27, 0:3, 0:8, 0:128]
    face_bytes = coef.at[0:14, 0:2, :, 0:128]

    def moved_by(array, b, c):
        if b:
            array = pltpu.roll(array, (-b) % 16, 1)
        if c:
            array = pltpu.roll(array, (-c) % 256, 2)
        return array

    def turn(array, planes):
        for n, (b, c) in enumerate(NEAR):
            moved[n, 0:planes] = moved_by(array, b, c)

    def apply(planes, first):
        total = jnp.zeros((planes, 16, 256), jnp.float32)
        for k in range(27):
            a = k // 9
            total = total + coef[k, first : first + planes] * moved[k % 9, a : a + planes]
        return total

    pltpu.make_async_copy(field_bytes, field_bytes, field_sem.at[0]).wait()
    lane_wide = lax.broadcasted_iota(jnp.int32, (8, 16, 128), 2)
    side = jnp.where(lane_wide < 64, field[1], field[2])
    turn(jnp.concatenate([field[0], side], axis=2), 8)

    pltpu.make_async_copy(edge_bytes, edge_bytes, edge_sem.at[0]).wait()
    merged = jnp.where((lane_wide[0:6] & 3) < 2, edge[1], edge[0])
    for k in range(27):
        coef[k, :, :, 128:256] = pltpu.roll(merged, (126 - 4 * k) % 128, 2)

    pltpu.make_async_copy(coef_bytes, coef_bytes, coef_sem.at[0]).wait()
    pltpu.make_async_copy(face_bytes, face_bytes, face_sem.at[0]).wait()
    for k in range(27):
        if k == 13:
            continue
        a, b, c = k // 9 - 1, k // 3 % 3 - 1, k % 3 - 1
        first = 0 if k > 13 else 4
        mirror = moved_by(coef[26 - k, first + a : first + a + 2], b, c)
        coef[k, first : first + 2, 0:8, 0:128] = mirror[:, 0:8, 0:128]

    one = apply(6, 0)
    turn(one, 6)
    two = apply(4, 1)
    turn(two, 4)
    three = jnp.zeros((2, 8, 128), jnp.float32)
    for k in range(27):
        a = k // 9
        three = three + coef[k, 2:4, 0:8, 0:128] * moved[k % 9, a : a + 2, 0:8, 0:128]
    own = [field[0, 3:5, 0:8, :], one[2:4, 0:8, 0:128], two[1:3, 0:8, 0:128], three]
    v = [[array[p] for p in range(2)] for array in own]

    tile = jnp.zeros((8, 128), jnp.float32)
    for k in range(6):
        i, j = k // 2, (k + 1) // 2
        product = v[i][0] * v[j][0] + v[i][1] * v[j][1]
        tile = jnp.where(row_id == k, jnp.sum(product, axis=0, keepdims=True), tile)
    for shift in (64, 32, 16):
        tile = tile + pltpu.roll(tile, shift, 1)
    row = jnp.sum(jnp.where((lane_id >> 4) == row_id, tile, 0.0), axis=0, keepdims=True)

    def spread(rows, here, offsets, sem):
        for o in offsets:
            pltpu.make_async_remote_copy(
                src_ref=rows.at[here],
                dst_ref=rows.at[here],
                send_sem=send_sem.at[0],
                recv_sem=sem,
                device_id=at(*o),
                device_id_type=MESH,
            ).start()
        count = len(offsets)
        pltpu.make_async_copy(rows.at[0:count], rows.at[0:count], sem).wait()

    here = gy * GZ + gz
    plane_rows[here] = row
    spread(plane_rows, here, plane_offsets, plane_sem.at[0])
    terms = [plane_rows[k] for k in range(PLANE)]
    while len(terms) > 1:
        terms = [terms[k] + terms[k + 1] for k in range(0, len(terms), 2)]
    line_rows[gx] = terms[0]
    pl.semaphore_wait(relay_8, 2)
    spread(line_rows, gx, line_offsets, line_sem.at[0])
    terms = [(line_rows[k], None) for k in range(GX)]
    terms = [two_sum(terms[k][0], terms[k + 1][0]) for k in range(0, GX, 2)]
    while len(terms) > 1:
        terms = [pair_add(terms[k], terms[k + 1]) for k in range(0, len(terms), 2)]
    pair = terms[0]
    for shift in (8, 4, 2, 1):
        pair = pair_add(pair, (pltpu.roll(pair[0], shift, 1), pltpu.roll(pair[1], shift, 1)))

    moments = [
        tuple(jnp.broadcast_to(part[:, 16 * k + 15 : 16 * k + 16], (8, 128)) for part in pair)
        for k in range(6)
    ]
    tau, x_coef, r_coef = conjugate(moments)
    for p in range(2):
        level = [v[k][p] for k in range(4)]
        basis = [level[0]]
        while len(level) > 1:
            level = [level[k + 1] - tau * level[k] for k in range(len(level) - 1)]
            basis.append(level[0])
        out[p] = x_coef[0] * basis[0] + x_coef[1] * basis[1] + x_coef[2] * basis[2]
        out[2 + p] = (
            r_coef[0] * basis[0] + r_coef[1] * basis[1] + r_coef[2] * basis[2] + r_coef[3] * basis[3]
        )

    for size in (field_bytes, edge_bytes, coef_bytes, face_bytes):
        pltpu.make_async_copy(size, size, send_sem.at[0]).wait()
    for rows, count in ((plane_rows, PLANE - 1), (line_rows, GX - 1)):
        pltpu.make_async_copy(rows.at[0:count], rows.at[0:count], send_sem.at[0]).wait()


def local(right_side, stencil, cool_table, cool_bin, cool_frac):
    both = pl.pallas_call(
        kernel,
        out_shape=jax.ShapeDtypeStruct((4, 8, 128), jnp.float32),
        in_specs=[pl.BlockSpec(memory_space=pl.ANY)] * 5,
        out_specs=pl.BlockSpec(memory_space=pltpu.VMEM),
        scratch_shapes=[
            pltpu.VMEM((27, 6, 16, 256), jnp.float32),
            pltpu.VMEM((2, 8, 128), jnp.float32),
            pltpu.VMEM((2, 6, 16, 128), jnp.float32),
            pltpu.VMEM((3, 8, 16, 128), jnp.float32),
            pltpu.VMEM((9, 8, 16, 256), jnp.float32),
            pltpu.VMEM((2, 128), jnp.float32),
            pltpu.VMEM((2, 8, 128), jnp.int32),
            pltpu.VMEM((2, 8, 128), jnp.float32),
            pltpu.VMEM((PLANE, 1, 128), jnp.float32),
            pltpu.VMEM((GX, 1, 128), jnp.float32),
            pltpu.SemaphoreType.DMA((5,)),
        ]
        + [pltpu.SemaphoreType.DMA((1,))] * 7
        + [pltpu.SemaphoreType.REGULAR] * 2,
        compiler_params=pltpu.CompilerParams(
            collective_id=0, has_side_effects=True, vmem_limit_bytes=60 << 20
        ),
    )(right_side, stencil, cool_table.reshape(2, 128), cool_bin, cool_frac)
    return both[0:2], both[2:4]


def solution(mesh):
    block = P("gx", "gy", "gz")
    return jax.shard_map(
        local,
        mesh=mesh,
        in_specs=(block, P(None, "gx", "gy", "gz"), P(), block, block),
        out_specs=(block, block),
        check_vma=False,
    )
```

```python
import functools
import jax
import jax.numpy as jnp
from jax import lax
from jax.experimental import pallas as pl
from jax.experimental.pallas import tpu as pltpu
from jax.sharding import PartitionSpec as P

MESH = pl.DeviceIdType.MESH
GX, GY, GZ = 32, 4, 8
PLANE = GY * GZ
SHIFT = 4.5
NEAR = [(b, c) for b in (-1, 0, 1) for c in (-1, 0, 1)]
FIELD_ROWS = {0: (0, 0, 8), 1: (5, 13, 3), -1: (0, 8, 3)}
COEF_ROWS = {0: (0, 0, 8), 1: (6, 14, 2), -1: (0, 8, 2)}
FIELD_PLANES = {0: (3, 3, 2), 1: (3, 1, 2), -1: (3, 5, 2), 2: (4, 0, 1), -2: (3, 7, 1)}
COEF_PLANES = {0: (2, 2), 1: (2, 0), -1: (2, 4)}
SIDE = {0: 0, 1: 2, -1: 1}
OUTWARD = {(1, -1): (15, 24), (1, 1): (18,), (-1, -1): (6,), (-1, 1): (0, 9)}


def two_sum(a, b):
    total = a + b
    part = total - a
    return total, (a - (total - part)) + (b - part)


def pair_add(x, y):
    total, error = two_sum(x[0], y[0])
    error = error + (x[1] + y[1])
    high = total + error
    return high, error - (high - total)


def halves(a):
    big = a * 4097.0
    high = big - (big - a)
    return high, a - high


def pair_minus_scaled(x, y, scale, scale_halves):
    product = y[0] * scale
    high, low = halves(y[0])
    scale_high, scale_low = scale_halves
    error = high * scale_high - product
    error = error + high * scale_low
    error = error + low * scale_high
    error = error + low * scale_low
    error = error + y[1] * scale
    return pair_add(x, (-product, -error))


def conjugate(moments):
    tau = moments[1][0] / moments[0][0]
    tau_halves = halves(tau)
    level = list(moments)
    shifted = [level[0][0]]
    while len(level) > 1:
        level = [
            pair_minus_scaled(level[k + 1], level[k], tau, tau_halves)
            for k in range(len(level) - 1)
        ]
        shifted.append(level[0][0])
    m = shifted
    s = tau + SHIFT

    def form(p, q):
        total = None
        for i, u in enumerate(p):
            inner = None
            for j, w in enumerate(q):
                term = w * m[i + j]
                inner = term if inner is None else inner + term
            total = u * inner if total is None else total + u * inner
        return total

    def image_of(p):
        out = [s * p[0]]
        for i in range(1, len(p)):
            out.append(p[i - 1] + s * p[i])
        out.append(p[-1])
        return out

    bottom = s * m[0] + m[1]
    alpha = m[0] / bottom
    x = [alpha]
    r = [m[1] / bottom, -alpha]
    norm = form(r, r)
    beta = norm / m[0]
    d = [r[0] + beta, r[1]]
    for step in (1, 2):
        image = image_of(d)
        alpha = norm / form(d, image)
        x = [x[i] + alpha * d[i] if i < len(x) else alpha * d[i] for i in range(len(d))]
        r = [r[i] - alpha * image[i] if i < len(r) else -alpha * image[i] for i in range(len(image))]
        if step == 1:
            new = form(r, r)
            beta = new / norm
            d = [r[i] + beta * d[i] if i < len(d) else r[i] for i in range(len(r))]
            norm = new
    return tau, x, r


def kernel(
    rhs_hbm, stencil_hbm, table_hbm, bin_hbm, frac_hbm, out,
    coef, packed, edge, field, side, own_strip, strips, moved, table, bins, frac, plane_rows, line_rows,
    in_sem, send_sem, field_sem, edge_sem, coef_sem, face_sem, plane_sem, line_sem,
    relay_4, relay_8,
):
    gx, gy, gz = lax.axis_index("gx"), lax.axis_index("gy"), lax.axis_index("gz")

    def at(dx, dy, dz):
        return (
            lax.rem(gx + (dx + GX), GX),
            lax.rem(gy + (dy + GY), GY),
            lax.rem(gz + (dz + GZ), GZ),
        )

    loads = [
        pltpu.make_async_copy(rhs_hbm, field.at[3:5, 0:8, :], in_sem.at[0]),
        pltpu.make_async_copy(stencil_hbm, coef.at[:, 2:4, 0:8, 0:128], in_sem.at[1]),
        pltpu.make_async_copy(table_hbm, table, in_sem.at[2]),
        pltpu.make_async_copy(bin_hbm, bins, in_sem.at[3]),
        pltpu.make_async_copy(frac_hbm, frac, in_sem.at[4]),
    ]
    for load in loads:
        load.start()

    plane_offsets = [(0, b, c) for b in range(GY) for c in range(GZ) if (b, c) != (0, 0)]
    line_offsets = [(a, 0, 0) for a in [16] + [k * e for k in range(15, 0, -1) for e in (1, -1)]]
    around = [(a, b, c) for a in (-2, 2, -1, 1) for b, c in NEAR if (b, c) != (0, 0)]
    around.sort(key=lambda o: -sum(abs(d) for d in o))
    partners = around + plane_offsets + [(a, 0, 0) for a in (4, -4, 3, -3, 2, -2, 1, -1)]
    barrier = pltpu.get_barrier_semaphore()
    for o in partners:
        pl.semaphore_signal(barrier, inc=1, device_id=at(*o), device_id_type=MESH)

    for load in loads:
        load.wait()

    low_tab = jnp.broadcast_to(table[0:1, :], (8, 128))
    high_tab = jnp.broadcast_to(table[1:2, :], (8, 128))

    def look(index):
        lane = index & 127
        low = jnp.take_along_axis(low_tab, lane, axis=1, mode="promise_in_bounds")
        high = jnp.take_along_axis(high_tab, lane, axis=1, mode="promise_in_bounds")
        return jnp.where(index >= 128, high, low)

    row_id = lax.broadcasted_iota(jnp.int32, (8, 128), 0)
    lane_id = lax.broadcasted_iota(jnp.int32, (8, 128), 1)
    for p in range(2):
        slope = look(bins[p]) * (1.0 - frac[p]) + look(bins[p] + 1) * frac[p]
        coef[13, 2 + p, 0:8, 0:128] = coef[13, 2 + p, 0:8, 0:128] + (slope - SHIFT)
        tile = jnp.zeros((8, 128), jnp.float32)
        for k in range(27):
            turned = pltpu.roll(coef[k, 2 + p, 0:8, 0:128], (4 * k + 2) % 128, 1)
            tile = jnp.where((lane_id >> 2) == k, turned, tile)
        packed[p] = tile

    strip = jnp.zeros((8, 128), jnp.float32)
    for p in range(2):
        ends = jnp.take_along_axis(
            field[3 + p, 0:8, :], ((lane_id & 7) + 125) & 127, axis=1, mode="promise_in_bounds"
        )
        strip = jnp.where((lane_id >> 3) == row_id + 8 * p, ends, strip)
    own_strip[0] = jnp.sum(strip, axis=0, keepdims=True)

    pl.semaphore_wait(barrier, len(partners))

    for a in (4, -4):
        pl.semaphore_signal(relay_4, inc=1, device_id=at(a, 0, 0), device_id_type=MESH)

    def send(src, dst, sem, o):
        pltpu.make_async_remote_copy(
            src_ref=src, dst_ref=dst, send_sem=send_sem.at[0], recv_sem=sem,
            device_id=at(*o), device_id_type=MESH,
        ).start()

    def send_field(dx, dy, dz):
        if dz:
            place = strips.at[SIDE[dz] - 1, 3 * (2 - dx) + (1 - dy)]
            send(own_strip.at[0], place, field_sem.at[0], (dx, dy, dz))
            return
        p_src, p_dst, p_n = FIELD_PLANES[dx]
        y_src, y_dst, y_n = FIELD_ROWS[dy]
        send(
            field.at[pl.ds(p_src, p_n), pl.ds(y_src, y_n), :],
            field.at[pl.ds(p_dst, p_n), pl.ds(y_dst, y_n), :],
            field_sem.at[0], (dx, dy, dz),
        )

    def send_edge(dx, dy, dz):
        p_src, p_dst = COEF_PLANES[dx]
        y_src, y_dst, y_n = COEF_ROWS[dy]
        send(
            packed.at[:, pl.ds(y_src, y_n), :],
            edge.at[SIDE[dz] - 1, pl.ds(p_dst, 2), pl.ds(y_dst, y_n), :],
            edge_sem.at[0], (dx, dy, dz),
        )

    def send_coef(dx, dy, first, count, sem, rows=None):
        p_src, p_dst = COEF_PLANES[dx]
        y_src, y_dst, y_n = rows or COEF_ROWS[dy]
        send(
            coef.at[pl.ds(first, count), pl.ds(p_src, 2), pl.ds(y_src, y_n), 0:128],
            coef.at[pl.ds(first, count), pl.ds(p_dst, 2), pl.ds(y_dst, y_n), 0:128],
            sem, (dx, dy, 0),
        )

    offsets = [(a, b, c) for a in (-1, 1, -2, 2, 0) for b, c in NEAR if (a, b, c) != (0, 0, 0)]
    offsets.sort(key=lambda o: -sum(abs(d) for d in o))
    for o in offsets:
        send_field(*o)
        if o[2] != 0 and abs(o[0]) <= 1:
            send_edge(*o)
    for dx in (-1, 1):
        half = 0 if dx == 1 else 13
        for dy in (-1, 1):
            send_coef(dx, dy, half, 14, coef_sem.at[0])
            for first in OUTWARD[dx, dy]:
                rows = (6, 14, 1) if dy == 1 else (1, 9, 1)
                send_coef(dx, dy, first, 3, coef_sem.at[0], rows)
    for dx in (-1, 1):
        send_coef(dx, 0, 0 if dx == 1 else 13, 14, face_sem.at[0])
    for dy in (-1, 1):
        send_coef(0, dy, 0, 27, coef_sem.at[0])

    pl.semaphore_wait(relay_4, 2)
    for a in (8, -8):
        pl.semaphore_signal(relay_8, inc=1, device_id=at(a, 0, 0), device_id_type=MESH)

    field_bytes = coef.at[0:9, 0:2, 0:7, 0:128]
    edge_bytes = coef.at[0:9, 0, :, 0:128]
    coef_bytes = coef.at[0:17, 0:4, 0:7, 0:128]
    face_bytes = coef.at[0:14, 0:2, :, 0:128]

    def moved_by(array, b, c):
        if b:
            array = pltpu.roll(array, (-b) % 16, 1)
        if c:
            array = pltpu.roll(array, (-c) % 256, 2)
        return array

    def turn(array, planes):
        for n, (b, c) in enumerate(NEAR):
            moved[n, 0:planes] = moved_by(array, b, c)

    def apply(planes, first):
        total = jnp.zeros((planes, 16, 256), jnp.float32)
        for k in range(27):
            a = k // 9
            total = total + coef[k, first : first + planes] * moved[k % 9, a : a + planes]
        return total

    pltpu.make_async_copy(field_bytes, field_bytes, field_sem.at[0]).wait()
    for plane in range(8):
        dx = (plane - 3) // 2
        first = 64 * ((plane - 3) % 2)
        line = lax.broadcasted_iota(jnp.int32, (1, 128), 1)

        def strip_of(dy):
            n = 3 * (dx + 2) + (dy + 1)
            return jnp.where((line & 7) < 3, strips[1, n], strips[0, n])

        source = [strip_of(0), jnp.where((line & 63) < 32, strip_of(1), strip_of(-1))]
        index = first + 8 * row_id + ((lane_id + 3) & 7)
        for n in range(2):
            side[plane, 8 * n : 8 * n + 8, :] = jnp.take_along_axis(
                jnp.broadcast_to(source[n], (8, 128)), index, axis=1, mode="promise_in_bounds"
            )
    turn(jnp.concatenate([field[...], side[...]], axis=2), 8)

    pltpu.make_async_copy(edge_bytes, edge_bytes, edge_sem.at[0]).wait()
    lane_wide = lax.broadcasted_iota(jnp.int32, (6, 16, 128), 2)
    merged = jnp.where((lane_wide & 3) < 2, edge[1], edge[0])
    for k in range(27):
        coef[k, :, :, 128:256] = pltpu.roll(merged, (126 - 4 * k) % 128, 2)

    pltpu.make_async_copy(coef_bytes, coef_bytes, coef_sem.at[0]).wait()
    pltpu.make_async_copy(face_bytes, face_bytes, face_sem.at[0]).wait()
    row_wide = lax.broadcasted_iota(jnp.int32, (2, 16, 128), 1)
    for k in range(27):
        if k == 13:
            continue
        a, b, c = k // 9 - 1, k // 3 % 3 - 1, k % 3 - 1
        first = 0 if k > 13 else 4
        mirror = moved_by(coef[26 - k, first + a : first + a + 2], b, c)[:, :, 0:128]
        if b:
            mirror = jnp.where(row_wide == (9 if b == 1 else 14), coef[k, first : first + 2, :, 0:128], mirror)
        coef[k, first : first + 2, :, 0:128] = mirror

    one = apply(6, 0)
    turn(one, 6)
    two = apply(4, 1)
    turn(two, 4)
    three = jnp.zeros((2, 8, 128), jnp.float32)
    for k in range(27):
        a = k // 9
        three = three + coef[k, 2:4, 0:8, 0:128] * moved[k % 9, a : a + 2, 0:8, 0:128]
    own = [field[3:5, 0:8, :], one[2:4, 0:8, 0:128], two[1:3, 0:8, 0:128], three]
    v = [[array[p] for p in range(2)] for array in own]

    tile = jnp.zeros((8, 128), jnp.float32)
    for k in range(6):
        i, j = k // 2, (k + 1) // 2
        product = v[i][0] * v[j][0] + v[i][1] * v[j][1]
        tile = jnp.where(row_id == k, jnp.sum(product, axis=0, keepdims=True), tile)
    for shift in (64, 32, 16):
        tile = tile + pltpu.roll(tile, shift, 1)
    row = jnp.sum(jnp.where((lane_id >> 4) == row_id, tile, 0.0), axis=0, keepdims=True)

    def spread(rows, here, offsets, sem):
        for o in offsets:
            pltpu.make_async_remote_copy(
                src_ref=rows.at[here],
                dst_ref=rows.at[here],
                send_sem=send_sem.at[0],
                recv_sem=sem,
                device_id=at(*o),
                device_id_type=MESH,
            ).start()
        count = len(offsets)
        pltpu.make_async_copy(rows.at[0:count], rows.at[0:count], sem).wait()

    here = gy * GZ + gz
    plane_rows[here] = row
    spread(plane_rows, here, plane_offsets, plane_sem.at[0])
    terms = [plane_rows[k] for k in range(PLANE)]
    while len(terms) > 1:
        terms = [terms[k] + terms[k + 1] for k in range(0, len(terms), 2)]
    line_rows[gx] = terms[0]
    pl.semaphore_wait(relay_8, 2)
    spread(line_rows, gx, line_offsets, line_sem.at[0])
    terms = [(line_rows[k], None) for k in range(GX)]
    terms = [two_sum(terms[k][0], terms[k + 1][0]) for k in range(0, GX, 2)]
    while len(terms) > 1:
        terms = [pair_add(terms[k], terms[k + 1]) for k in range(0, len(terms), 2)]
    pair = terms[0]
    for shift in (8, 4, 2, 1):
        pair = pair_add(pair, (pltpu.roll(pair[0], shift, 1), pltpu.roll(pair[1], shift, 1)))

    moments = [
        tuple(jnp.broadcast_to(part[:, 16 * k + 15 : 16 * k + 16], (8, 128)) for part in pair)
        for k in range(6)
    ]
    tau, x_coef, r_coef = conjugate(moments)
    for p in range(2):
        level = [v[k][p] for k in range(4)]
        basis = [level[0]]
        while len(level) > 1:
            level = [level[k + 1] - tau * level[k] for k in range(len(level) - 1)]
            basis.append(level[0])
        out[p] = x_coef[0] * basis[0] + x_coef[1] * basis[1] + x_coef[2] * basis[2]
        out[2 + p] = (
            r_coef[0] * basis[0] + r_coef[1] * basis[1] + r_coef[2] * basis[2] + r_coef[3] * basis[3]
        )

    for size in (field_bytes, edge_bytes, coef_bytes, face_bytes):
        pltpu.make_async_copy(size, size, send_sem.at[0]).wait()
    for rows, count in ((plane_rows, PLANE - 1), (line_rows, GX - 1)):
        pltpu.make_async_copy(rows.at[0:count], rows.at[0:count], send_sem.at[0]).wait()


def local(right_side, stencil, cool_table, cool_bin, cool_frac):
    both = pl.pallas_call(
        kernel,
        out_shape=jax.ShapeDtypeStruct((4, 8, 128), jnp.float32),
        in_specs=[pl.BlockSpec(memory_space=pl.ANY)] * 5,
        out_specs=pl.BlockSpec(memory_space=pltpu.VMEM),
        scratch_shapes=[
            pltpu.VMEM((27, 6, 16, 256), jnp.float32),
            pltpu.VMEM((2, 8, 128), jnp.float32),
            pltpu.VMEM((2, 6, 16, 128), jnp.float32),
            pltpu.VMEM((8, 16, 128), jnp.float32),
            pltpu.VMEM((8, 16, 128), jnp.float32),
            pltpu.VMEM((1, 1, 128), jnp.float32),
            pltpu.VMEM((2, 15, 1, 128), jnp.float32),
            pltpu.VMEM((9, 8, 16, 256), jnp.float32),
            pltpu.VMEM((2, 128), jnp.float32),
            pltpu.VMEM((2, 8, 128), jnp.int32),
            pltpu.VMEM((2, 8, 128), jnp.float32),
            pltpu.VMEM((PLANE, 1, 128), jnp.float32),
            pltpu.VMEM((GX, 1, 128), jnp.float32),
            pltpu.SemaphoreType.DMA((5,)),
        ]
        + [pltpu.SemaphoreType.DMA((1,))] * 7
        + [pltpu.SemaphoreType.REGULAR] * 2,
        compiler_params=pltpu.CompilerParams(
            collective_id=0, has_side_effects=True, vmem_limit_bytes=60 << 20
        ),
    )(right_side, stencil, cool_table.reshape(2, 128), cool_bin, cool_frac)
    return both[0:2], both[2:4]


def solution(mesh):
    block = P("gx", "gy", "gz")
    return jax.shard_map(
        local,
        mesh=mesh,
        in_specs=(block, P(None, "gx", "gy", "gz"), P(), block, block),
        out_specs=(block, block),
        check_vma=False,
    )
```

```python
import functools
import jax
import jax.numpy as jnp
from jax import lax
from jax.experimental import pallas as pl
from jax.experimental.pallas import tpu as pltpu
from jax.sharding import PartitionSpec as P

MESH = pl.DeviceIdType.MESH
GX, GY, GZ = 32, 4, 8
PLANE = GY * GZ
SHIFT = 4.5
NEAR = [(b, c) for b in (-1, 0, 1) for c in (-1, 0, 1)]
FIELD_ROWS = {0: (0, 0, 8), 1: (5, 13, 3), -1: (0, 8, 3)}
COEF_ROWS = {0: (0, 0, 8), 1: (6, 14, 2), -1: (0, 8, 2)}
FIELD_PLANES = {0: (3, 3, 2), 1: (3, 1, 2), -1: (3, 5, 2), 2: (4, 0, 1), -2: (3, 7, 1)}
COEF_PLANES = {0: (2, 2), 1: (2, 0), -1: (2, 4)}
SIDE = {0: 0, 1: 2, -1: 1}
OUTWARD = {(1, -1): (15, 24), (1, 1): (18,), (-1, -1): (6,), (-1, 1): (0, 9)}


def two_sum(a, b):
    total = a + b
    part = total - a
    return total, (a - (total - part)) + (b - part)


def pair_add(x, y):
    total, error = two_sum(x[0], y[0])
    error = error + (x[1] + y[1])
    high = total + error
    return high, error - (high - total)


def halves(a):
    big = a * 4097.0
    high = big - (big - a)
    return high, a - high


def pair_minus_scaled(x, y, scale, scale_halves):
    product = y[0] * scale
    high, low = halves(y[0])
    scale_high, scale_low = scale_halves
    error = high * scale_high - product
    error = error + high * scale_low
    error = error + low * scale_high
    error = error + low * scale_low
    error = error + y[1] * scale
    return pair_add(x, (-product, -error))


def conjugate(moments):
    tau = moments[1][0] / moments[0][0]
    tau_halves = halves(tau)
    level = list(moments)
    shifted = [level[0][0]]
    while len(level) > 1:
        level = [
            pair_minus_scaled(level[k + 1], level[k], tau, tau_halves)
            for k in range(len(level) - 1)
        ]
        shifted.append(level[0][0])
    m = shifted
    s = tau + SHIFT

    def form(p, q):
        total = None
        for i, u in enumerate(p):
            inner = None
            for j, w in enumerate(q):
                term = w * m[i + j]
                inner = term if inner is None else inner + term
            total = u * inner if total is None else total + u * inner
        return total

    def image_of(p):
        out = [s * p[0]]
        for i in range(1, len(p)):
            out.append(p[i - 1] + s * p[i])
        out.append(p[-1])
        return out

    bottom = s * m[0] + m[1]
    alpha = m[0] / bottom
    x = [alpha]
    r = [m[1] / bottom, -alpha]
    norm = form(r, r)
    beta = norm / m[0]
    d = [r[0] + beta, r[1]]
    for step in (1, 2):
        image = image_of(d)
        alpha = norm / form(d, image)
        x = [x[i] + alpha * d[i] if i < len(x) else alpha * d[i] for i in range(len(d))]
        r = [r[i] - alpha * image[i] if i < len(r) else -alpha * image[i] for i in range(len(image))]
        if step == 1:
            new = form(r, r)
            beta = new / norm
            d = [r[i] + beta * d[i] if i < len(d) else r[i] for i in range(len(r))]
            norm = new
    return tau, x, r


def kernel(
    rhs_hbm, stencil_hbm, table_hbm, bin_hbm, frac_hbm, out,
    coef, packed, edge, field, side, own_strip, strips, moved, table, bins, frac, plane_rows, line_rows,
    in_sem, send_sem, field_sem, edge_sem, coef_sem, face_sem, row_sem, plane_sem, line_sem,
    relay_4, relay_8,
):
    gx, gy, gz = lax.axis_index("gx"), lax.axis_index("gy"), lax.axis_index("gz")

    def at(dx, dy, dz):
        return (
            lax.rem(gx + (dx + GX), GX),
            lax.rem(gy + (dy + GY), GY),
            lax.rem(gz + (dz + GZ), GZ),
        )

    loads = [
        pltpu.make_async_copy(rhs_hbm, field.at[3:5, 0:8, :], in_sem.at[0]),
        pltpu.make_async_copy(stencil_hbm, coef.at[:, 2:4, 0:8, 0:128], in_sem.at[1]),
        pltpu.make_async_copy(table_hbm, table, in_sem.at[2]),
        pltpu.make_async_copy(bin_hbm, bins, in_sem.at[3]),
        pltpu.make_async_copy(frac_hbm, frac, in_sem.at[4]),
    ]
    for load in loads:
        load.start()

    plane_offsets = [(0, b, c) for b in range(GY) for c in range(GZ) if (b, c) != (0, 0)]
    plane_offsets.sort(key=lambda o: -(min(o[1], GY - o[1]) + min(o[2], GZ - o[2]) / 2))
    line_offsets = [(a, 0, 0) for a in [16] + [k * e for k in range(15, 0, -1) for e in (1, -1)]]
    around = [(a, b, c) for a in (-2, 2, -1, 1) for b, c in NEAR if (b, c) != (0, 0)]
    around.sort(key=lambda o: -sum(abs(d) for d in o))
    partners = around + plane_offsets + [(a, 0, 0) for a in (4, -4, 3, -3, 2, -2, 1, -1)]
    barrier = pltpu.get_barrier_semaphore()
    for o in partners:
        pl.semaphore_signal(barrier, inc=1, device_id=at(*o), device_id_type=MESH)

    for load in loads:
        load.wait()

    low_tab = jnp.broadcast_to(table[0:1, :], (8, 128))
    high_tab = jnp.broadcast_to(table[1:2, :], (8, 128))

    def look(index):
        lane = index & 127
        low = jnp.take_along_axis(low_tab, lane, axis=1, mode="promise_in_bounds")
        high = jnp.take_along_axis(high_tab, lane, axis=1, mode="promise_in_bounds")
        return jnp.where(index >= 128, high, low)

    row_id = lax.broadcasted_iota(jnp.int32, (8, 128), 0)
    lane_id = lax.broadcasted_iota(jnp.int32, (8, 128), 1)
    for p in range(2):
        slope = look(bins[p]) * (1.0 - frac[p]) + look(bins[p] + 1) * frac[p]
        coef[13, 2 + p, 0:8, 0:128] = coef[13, 2 + p, 0:8, 0:128] + (slope - SHIFT)
        tile = jnp.zeros((8, 128), jnp.float32)
        for k in range(27):
            turned = pltpu.roll(coef[k, 2 + p, 0:8, 0:128], (4 * k + 2) % 128, 1)
            tile = jnp.where((lane_id >> 2) == k, turned, tile)
        packed[p] = tile

    strip = jnp.zeros((8, 128), jnp.float32)
    for p in range(2):
        ends = jnp.take_along_axis(
            field[3 + p, 0:8, :], ((lane_id & 7) + 125) & 127, axis=1, mode="promise_in_bounds"
        )
        strip = jnp.where((lane_id >> 3) == row_id + 8 * p, ends, strip)
    own_strip[0] = jnp.sum(strip, axis=0, keepdims=True)

    pl.semaphore_wait(barrier, len(partners))

    for a in (4, -4):
        pl.semaphore_signal(relay_4, inc=1, device_id=at(a, 0, 0), device_id_type=MESH)

    def send(src, dst, sem, o):
        pltpu.make_async_remote_copy(
            src_ref=src, dst_ref=dst, send_sem=send_sem.at[0], recv_sem=sem,
            device_id=at(*o), device_id_type=MESH,
        ).start()

    def send_field(dx, dy, dz):
        if dz:
            place = strips.at[SIDE[dz] - 1, 3 * (2 - dx) + (1 - dy)]
            send(own_strip.at[0], place, field_sem.at[0], (dx, dy, dz))
            return
        p_src, p_dst, p_n = FIELD_PLANES[dx]
        y_src, y_dst, y_n = FIELD_ROWS[dy]
        send(
            field.at[pl.ds(p_src, p_n), pl.ds(y_src, y_n), :],
            field.at[pl.ds(p_dst, p_n), pl.ds(y_dst, y_n), :],
            field_sem.at[0], (dx, dy, dz),
        )

    def send_edge(dx, dy, dz):
        p_src, p_dst = COEF_PLANES[dx]
        y_src, y_dst, y_n = COEF_ROWS[dy]
        send(
            packed.at[:, pl.ds(y_src, y_n), :],
            edge.at[SIDE[dz] - 1, pl.ds(p_dst, 2), pl.ds(y_dst, y_n), :],
            edge_sem.at[0], (dx, dy, dz),
        )

    def send_coef(dx, dy, first, count, sem, rows=None):
        p_src, p_dst = COEF_PLANES[dx]
        y_src, y_dst, y_n = rows or COEF_ROWS[dy]
        send(
            coef.at[pl.ds(first, count), pl.ds(p_src, 2), pl.ds(y_src, y_n), 0:128],
            coef.at[pl.ds(first, count), pl.ds(p_dst, 2), pl.ds(y_dst, y_n), 0:128],
            sem, (dx, dy, 0),
        )

    offsets = [(a, b, c) for a in (-1, 1, -2, 2, 0) for b, c in NEAR if (a, b, c) != (0, 0, 0)]
    offsets.sort(key=lambda o: -sum(abs(d) for d in o))
    for o in offsets:
        send_field(*o)
        if o[2] != 0 and abs(o[0]) <= 1:
            send_edge(*o)
    for dy in (-1, 1):
        send_coef(0, dy, 0, 27, row_sem.at[0])
    for dx in (-1, 1):
        half = 0 if dx == 1 else 13
        for dy in (-1, 1):
            send_coef(dx, dy, half, 14, coef_sem.at[0])
            for first in OUTWARD[dx, dy]:
                rows = (6, 14, 1) if dy == 1 else (1, 9, 1)
                send_coef(dx, dy, first, 3, coef_sem.at[0], rows)
    for dx in (-1, 1):
        send_coef(dx, 0, 0 if dx == 1 else 13, 14, face_sem.at[0])

    pl.semaphore_wait(relay_4, 2)
    for a in (8, -8):
        pl.semaphore_signal(relay_8, inc=1, device_id=at(a, 0, 0), device_id_type=MESH)

    field_bytes = coef.at[0:9, 0:2, 0:7, 0:128]
    edge_bytes = coef.at[0:9, 0, :, 0:128]
    coef_bytes = coef.at[0:13, 0:4, 0:5, 0:128]
    row_bytes = coef.at[0:27, 0, 0:8, 0:128]
    face_bytes = coef.at[0:14, 0:2, :, 0:128]

    def moved_by(array, b, c):
        if b:
            array = pltpu.roll(array, (-b) % 16, 1)
        if c:
            array = pltpu.roll(array, (-c) % 256, 2)
        return array

    def turn(array, planes):
        for n, (b, c) in enumerate(NEAR):
            moved[n, 0:planes] = moved_by(array, b, c)

    def apply(planes, first, base=None):
        base = first if base is None else base
        total = jnp.zeros((planes, 16, 256), jnp.float32)
        for k in range(27):
            a = k // 9
            total = total + coef[k, first : first + planes] * moved[k % 9, first - base + a : first - base + a + planes]
        return total

    pltpu.make_async_copy(field_bytes, field_bytes, field_sem.at[0]).wait()
    for plane in range(8):
        dx = (plane - 3) // 2
        first = 64 * ((plane - 3) % 2)
        line = lax.broadcasted_iota(jnp.int32, (1, 128), 1)

        def strip_of(dy):
            n = 3 * (dx + 2) + (dy + 1)
            return jnp.where((line & 7) < 3, strips[1, n], strips[0, n])

        source = [strip_of(0), jnp.where((line & 63) < 32, strip_of(1), strip_of(-1))]
        index = first + 8 * row_id + ((lane_id + 3) & 7)
        for n in range(2):
            side[plane, 8 * n : 8 * n + 8, :] = jnp.take_along_axis(
                jnp.broadcast_to(source[n], (8, 128)), index, axis=1, mode="promise_in_bounds"
            )
    turn(jnp.concatenate([field[...], side[...]], axis=2), 8)

    pltpu.make_async_copy(edge_bytes, edge_bytes, edge_sem.at[0]).wait()
    lane_wide = lax.broadcasted_iota(jnp.int32, (6, 16, 128), 2)
    merged = jnp.where((lane_wide & 3) < 2, edge[1], edge[0])
    for k in range(27):
        coef[k, :, :, 128:256] = pltpu.roll(merged, (126 - 4 * k) % 128, 2)

    pltpu.make_async_copy(row_bytes, row_bytes, row_sem.at[0]).wait()
    middle = apply(2, 2, 0)

    pltpu.make_async_copy(coef_bytes, coef_bytes, coef_sem.at[0]).wait()
    pltpu.make_async_copy(face_bytes, face_bytes, face_sem.at[0]).wait()
    row_wide = lax.broadcasted_iota(jnp.int32, (2, 16, 128), 1)
    for k in range(27):
        if k == 13:
            continue
        a, b, c = k // 9 - 1, k // 3 % 3 - 1, k % 3 - 1
        first = 0 if k > 13 else 4
        mirror = moved_by(coef[26 - k, first + a : first + a + 2], b, c)[:, :, 0:128]
        if b:
            mirror = jnp.where(row_wide == (9 if b == 1 else 14), coef[k, first : first + 2, :, 0:128], mirror)
        coef[k, first : first + 2, :, 0:128] = mirror

    one = jnp.concatenate([apply(2, 0, 0), middle, apply(2, 4, 0)], axis=0)
    turn(one, 6)
    two = apply(4, 1)
    turn(two, 4)
    three = jnp.zeros((2, 8, 128), jnp.float32)
    for k in range(27):
        a = k // 9
        three = three + coef[k, 2:4, 0:8, 0:128] * moved[k % 9, a : a + 2, 0:8, 0:128]
    own = [field[3:5, 0:8, :], one[2:4, 0:8, 0:128], two[1:3, 0:8, 0:128], three]
    v = [[array[p] for p in range(2)] for array in own]

    tile = jnp.zeros((8, 128), jnp.float32)
    for k in range(6):
        i, j = k // 2, (k + 1) // 2
        product = v[i][0] * v[j][0] + v[i][1] * v[j][1]
        tile = jnp.where(row_id == k, jnp.sum(product, axis=0, keepdims=True), tile)
    for shift in (64, 32, 16):
        tile = tile + pltpu.roll(tile, shift, 1)
    row = jnp.sum(jnp.where((lane_id >> 4) == row_id, tile, 0.0), axis=0, keepdims=True)

    def spread(rows, here, offsets, sem):
        for o in offsets:
            pltpu.make_async_remote_copy(
                src_ref=rows.at[here],
                dst_ref=rows.at[here],
                send_sem=send_sem.at[0],
                recv_sem=sem,
                device_id=at(*o),
                device_id_type=MESH,
            ).start()
        count = len(offsets)
        pltpu.make_async_copy(rows.at[0:count], rows.at[0:count], sem).wait()

    here = gy * GZ + gz
    plane_rows[here] = row
    spread(plane_rows, here, plane_offsets, plane_sem.at[0])
    terms = [plane_rows[k] for k in range(PLANE)]
    while len(terms) > 1:
        terms = [terms[k] + terms[k + 1] for k in range(0, len(terms), 2)]
    line_rows[gx] = terms[0]
    pl.semaphore_wait(relay_8, 2)
    spread(line_rows, gx, line_offsets, line_sem.at[0])
    terms = [(line_rows[k], None) for k in range(GX)]
    terms = [two_sum(terms[k][0], terms[k + 1][0]) for k in range(0, GX, 2)]
    while len(terms) > 1:
        terms = [pair_add(terms[k], terms[k + 1]) for k in range(0, len(terms), 2)]
    pair = terms[0]
    for shift in (8, 4, 2, 1):
        pair = pair_add(pair, (pltpu.roll(pair[0], shift, 1), pltpu.roll(pair[1], shift, 1)))

    moments = [
        tuple(jnp.broadcast_to(part[:, 16 * k + 15 : 16 * k + 16], (8, 128)) for part in pair)
        for k in range(6)
    ]
    tau, x_coef, r_coef = conjugate(moments)
    for p in range(2):
        level = [v[k][p] for k in range(4)]
        basis = [level[0]]
        while len(level) > 1:
            level = [level[k + 1] - tau * level[k] for k in range(len(level) - 1)]
            basis.append(level[0])
        out[p] = x_coef[0] * basis[0] + x_coef[1] * basis[1] + x_coef[2] * basis[2]
        out[2 + p] = (
            r_coef[0] * basis[0] + r_coef[1] * basis[1] + r_coef[2] * basis[2] + r_coef[3] * basis[3]
        )

    for size in (field_bytes, edge_bytes, row_bytes, coef_bytes, face_bytes):
        pltpu.make_async_copy(size, size, send_sem.at[0]).wait()
    for rows, count in ((plane_rows, PLANE - 1), (line_rows, GX - 1)):
        pltpu.make_async_copy(rows.at[0:count], rows.at[0:count], send_sem.at[0]).wait()


def local(right_side, stencil, cool_table, cool_bin, cool_frac):
    both = pl.pallas_call(
        kernel,
        out_shape=jax.ShapeDtypeStruct((4, 8, 128), jnp.float32),
        in_specs=[pl.BlockSpec(memory_space=pl.ANY)] * 5,
        out_specs=pl.BlockSpec(memory_space=pltpu.VMEM),
        scratch_shapes=[
            pltpu.VMEM((27, 6, 16, 256), jnp.float32),
            pltpu.VMEM((2, 8, 128), jnp.float32),
            pltpu.VMEM((2, 6, 16, 128), jnp.float32),
            pltpu.VMEM((8, 16, 128), jnp.float32),
            pltpu.VMEM((8, 16, 128), jnp.float32),
            pltpu.VMEM((1, 1, 128), jnp.float32),
            pltpu.VMEM((2, 15, 1, 128), jnp.float32),
            pltpu.VMEM((9, 8, 16, 256), jnp.float32),
            pltpu.VMEM((2, 128), jnp.float32),
            pltpu.VMEM((2, 8, 128), jnp.int32),
            pltpu.VMEM((2, 8, 128), jnp.float32),
            pltpu.VMEM((PLANE, 1, 128), jnp.float32),
            pltpu.VMEM((GX, 1, 128), jnp.float32),
            pltpu.SemaphoreType.DMA((5,)),
        ]
        + [pltpu.SemaphoreType.DMA((1,))] * 8
        + [pltpu.SemaphoreType.REGULAR] * 2,
        compiler_params=pltpu.CompilerParams(
            collective_id=0, has_side_effects=True, vmem_limit_bytes=60 << 20
        ),
    )(right_side, stencil, cool_table.reshape(2, 128), cool_bin, cool_frac)
    return both[0:2], both[2:4]


def solution(mesh):
    block = P("gx", "gy", "gz")
    return jax.shard_map(
        local,
        mesh=mesh,
        in_specs=(block, P(None, "gx", "gy", "gz"), P(), block, block),
        out_specs=(block, block),
        check_vma=False,
    )
```
